32 devices in a mesh: band: 16 (over z, y, x), slab: 2 (over core).
Axes of the slice: x: 2, y: 2, z: 4, core: 2. Of those that a mesh axis runs over, the one named last changes fastest.
Arguments:
- feats: bfloat16 [2, 2048, 128], P('slab', 'band'), may hold values from -6 to 6
- nbrs: int32 [2, 2048, 16], P('slab', 'band'), may hold values from 0 to 2047
- w_pair: bfloat16 [128, 512], replicated, may hold values from -0.5 to 0.5
- stiff: float32 [4096], P('band'), may hold values from 0.5 to 2
- order: int32 [16], replicated, may hold values from 0 to 15, each once
Outputs:
- schur: float32 [2, 2048, 16, 256], P('slab', None, 'band')
- log_mean: float32 [], replicated
The draws below stay inside these ranges and needn't reach their ends.
Inputs may be any that keep to these rules, and one draw needn't show every extreme that they name: `nbrs`: neighbours lie in the bead's own slab group. `order`: each column block appears once.
All inputs are finite; a program needn't handle non-finite values.
Results may differ from the reference program's by a relative error of at most 0.01.
Values may be sent and summed in bfloat16 or wider, within the bound.
A program may use at most 64 MiB of HBM per device.

```python
import math
import jax
import jax.numpy as jnp
from jax import lax

B = 256
E = 128
C = 512
NBR = 16
STEPS = 1
W = 4096
SLAB_ROWS = 2048
N_BAND = 16
N_SLAB = 2


def place_ends(result, rng, least, high):
    longest = result.shape.index(max(result.shape))
    spots = []
    for shift in (0, 1):
        where = [jax.random.randint(jax.random.fold_in(rng, axis), (), 0, length) for axis, length in enumerate(result.shape)]
        where[longest] = (where[longest] + shift) % result.shape[longest]
        spots.append(tuple(where))
    return result.at[spots[0]].set(least).at[spots[1]].set(high)


def shard_levels(stream_key, shape, shards, least, high):
    gain = 1.0
    for axis_at, blocks in shards:
        draws = jax.random.uniform(jax.random.fold_in(jax.random.fold_in(stream_key, 6), axis_at), (blocks,), jnp.float32, least / len(shards), high / len(shards))
        gain = gain * jnp.repeat(jnp.exp(draws), shape[axis_at] // blocks).reshape((-1,) + (1,) * (len(shape) - 1 - axis_at))
    return gain


def scatter_about(rng, shape, scale, limit, cuts=(), held_as=jnp.bfloat16):
    level = shard_levels(rng, shape, cuts, -0.22, 0.18) if cuts else 1.0
    values = jax.random.normal(rng, shape, jnp.float32) * scale * level
    return jnp.minimum(jnp.maximum(values, -limit), limit).astype(held_as)


def setup_inputs(seed: int = 0) -> dict:
    streams_of = jax.random.split(jax.random.key(seed), 6)
    feats = scatter_about(streams_of[0], (N_SLAB, SLAB_ROWS, E), 1.0, 6.0, ((0, 2), (1, 16)))
    nbrs = place_ends(jax.random.randint(streams_of[1], (N_SLAB, SLAB_ROWS, NBR), 0, SLAB_ROWS), jax.random.fold_in(streams_of[1], 1), 0, SLAB_ROWS - 1).astype(jnp.int32)
    w_pair = scatter_about(streams_of[2], (E, C), E ** -0.5, 0.5)
    stiff = jnp.clip(jnp.exp(math.log(2.0) - 1.3862944 * jax.random.uniform(streams_of[3], (W,), jnp.float32) ** shard_levels(streams_of[3], (W,), ((0, 16),), -0.2, 0.2)), 0.5, 2.0)
    order = jax.random.permutation(streams_of[4], N_BAND).astype(jnp.int32)
    return {"feats": feats, "nbrs": nbrs, "w_pair": w_pair, "stiff": stiff, "order": order}


def pair_factor(rows_feats, rows_nbrs, slab_feats, w_pair):
    count = rows_feats.shape[0]
    width = min(count, 128)
    blocks = count // width
    scale = 1.5 / math.sqrt(rows_nbrs.shape[1] * w_pair.shape[1])

    def one_block(pieces):
        own, links = pieces
        near = jnp.take(slab_feats, links, axis=0)
        mixed = (own[:, None, :].astype(jnp.float32) * near.astype(jnp.float32)).astype(jnp.bfloat16)
        pre = jnp.einsum('rne,ec->rnc', mixed.astype(jnp.float32), w_pair.astype(jnp.float32))
        return (lax.optimization_barrier(jnp.sum(jnp.tanh(pre), axis=1)) * scale).astype(jnp.bfloat16)
    out = lax.map(one_block, (rows_feats.reshape(blocks, width, -1), rows_nbrs.reshape(blocks, width, -1)))
    return out.reshape(count, -1)

def reference(feats, nbrs, w_pair, stiff, order):
    groups = feats.shape[0]
    block = B
    width = N_BAND * B
    factors = lax.map(lambda pieces: pair_factor(pieces[0], pieces[1], pieces[0], w_pair), (feats, nbrs))
    rows_per = factors.shape[1] // block
    natural = factors.reshape(groups, rows_per, block, -1).transpose(1, 0, 2, 3).reshape(width, -1).astype(jnp.float32)
    matrix = jnp.dot(natural, natural.T, precision=lax.Precision.HIGHEST)
    places = jnp.arange(width)
    matrix = matrix.at[places, places].add(stiff)
    block_ids = (jnp.arange(width) // block).astype(jnp.int32)
    total = jnp.zeros((), jnp.float32)
    for step in range(STEPS):
        pivot = order[step].astype(jnp.int32)
        start = (pivot * block).astype(jnp.int32)
        column = lax.dynamic_slice_in_dim(matrix, start, block, 1)
        diag_block = lax.dynamic_slice_in_dim(column, start, block, 0)
        lower = jnp.linalg.cholesky(diag_block)
        solved = lax.linalg.triangular_solve(lower, column, left_side=False, lower=True, transpose_a=True)
        done = jnp.any(block_ids[:, None] == order[:step + 1].astype(jnp.int32)[None, :], axis=1)
        rounded = jnp.where(done[:, None], 0.0, solved).astype(jnp.bfloat16)
        rounded = lax.optimization_barrier(rounded)
        panel = rounded.astype(jnp.float32)
        matrix = matrix - jnp.dot(panel, panel.T, precision=lax.Precision.HIGHEST)
        total = total + 2.0 * jnp.sum(jnp.log(jnp.diagonal(lower)))
    schur = matrix.reshape(rows_per, groups, block, width).transpose(1, 0, 2, 3).reshape(groups, rows_per * block, N_BAND, block)
    return (schur, total / (STEPS * block))
```

```python
import functools
import math

import jax
import jax.numpy as jnp
from jax import lax
from jax.experimental import pallas as pl
from jax.experimental.pallas import tpu as pltpu
from jax.sharding import PartitionSpec as P

STEPS = 1
MESH = pl.DeviceIdType.MESH
TAIL = 16
HI = lax.Precision.HIGHEST


def slots(buf, origin, rows, piece):
    start, size = piece
    return buf.at[pl.ds(pl.multiple_of(origin * rows + start, 16), size), :]


def tree_gather(n, me, buf, rows, pieces, send_sem, recv_sem):
    depth = n // 4
    z, y, x = me // 4, (me // 2) % 2, me % 2
    xn = me + 1 - 2 * x
    yn = me + 2 - 4 * y
    xyn = xn + 2 - 4 * y
    targets = (me + 4, me - 4, xn, yn)
    sent = []

    def copy(origin, piece, way):
        block = slots(buf, origin, rows, pieces[piece])
        return pltpu.make_async_remote_copy(
            src_ref=block,
            dst_ref=block,
            send_sem=send_sem.at[(origin * 2 + piece) * 4 + way],
            recv_sem=recv_sem.at[origin * 2 + piece],
            device_id={"band": targets[way]},
            device_id_type=MESH,
        )

    def send(origin, piece, way, cond):
        sent.append((origin, piece, way, cond))
        if cond is None:
            copy(origin, piece, way).start()
        else:
            pl.when(cond)(lambda: copy(origin, piece, way).start())

    def arrived(origin, piece, cond):
        if cond is None:
            copy(origin, piece, 2).wait_recv()
        else:
            pl.when(cond)(lambda: copy(origin, piece, 2).wait_recv())

    def both(a, b):
        return b if a is None else jnp.logical_and(a, b)

    def exists(dz):
        if dz == 0:
            return None
        return z < depth - dz if dz > 0 else z >= -dz

    def line(dz):
        cond = exists(dz)
        origin = me + 4 * dz
        for piece in (0, 1):
            if dz:
                arrived(origin, piece, cond)
            if dz <= 0:
                send(origin, piece, 0, both(cond, z < depth - 1))
            if dz >= 0:
                send(origin, piece, 1, both(cond, z > 0))
            for way in (2 + piece, 3 - piece):
                send(origin, piece, way, cond)

    def side(dz):
        cond = exists(dz)
        arrived(xn + 4 * dz, 0, cond)
        send(xn + 4 * dz, 0, 3, cond)
        arrived(yn + 4 * dz, 1, cond)
        send(yn + 4 * dz, 1, 2, cond)

    line(0)
    for far in range(1, depth + 1):
        if far < depth:
            line(far)
            line(-far)
        side(far - 1)
        if far > 1:
            side(1 - far)
    for dz in range(1 - depth, depth):
        cond = exists(dz)
        arrived(yn + 4 * dz, 0, cond)
        arrived(xyn + 4 * dz, 0, cond)
        arrived(xn + 4 * dz, 1, cond)
        arrived(xyn + 4 * dz, 1, cond)

    def drain():
        for origin, piece, way, cond in sent:
            if cond is None:
                copy(origin, piece, way).wait_send()
            else:
                pl.when(cond)(functools.partial(lambda o, p, w: copy(o, p, w).wait_send(), origin, piece, way))

    return drain


def direct_gather(n, me, buf, rows, pieces, send_sem, recv_sem):
    whole = (0, sum(size for _, size in pieces))

    def copy(origin, shift):
        block = slots(buf, origin, rows, whole)
        return pltpu.make_async_remote_copy(
            src_ref=block,
            dst_ref=block,
            send_sem=send_sem.at[shift],
            recv_sem=recv_sem.at[shift],
            device_id={"band": lax.rem(me + shift, n)},
            device_id_type=MESH,
        )

    @pl.loop(1, n)
    def _(shift):
        copy(me, shift).start()

    @pl.loop(1, n)
    def _(shift):
        copy(lax.rem(me + n - shift, n), shift).wait_recv()

    def drain():
        @pl.loop(1, n)
        def _(shift):
            copy(me, shift).wait_send()

    return drain


def assemble_kernel(
    n, groups, block, scale,
    order_ref, nbrs_ref, feats_ref, w_ref, stiff_ref,
    slab_ref, column_ref, pivot_ref, pstiff_ref,
    gathered, wide, near, pivots,
    fsend, frecv, ssend, srecv, csend, crecv, psend, precv,
):
    me = lax.axis_index("band")
    slab = lax.axis_index("slab")
    beads = feats_ref.shape[0]
    links = nbrs_ref.shape[0] // beads
    frows = beads + TAIL
    tree = n == 16
    gather = tree_gather if tree else direct_gather
    home = me // groups
    owner = lax.rem(me, groups)

    barrier = pltpu.get_barrier_semaphore()
    if tree:
        z, y, x = me // 4, (me // 2) % 2, me % 2
        mates = [(me + 1 - 2 * x, None), (me + 2 - 4 * y, None), (me + 4, z < n // 4 - 1), (me - 4, z > 0)]
        for mate, cond in mates:
            def greet(mate=mate):
                pl.semaphore_signal(barrier, inc=1, device_id={"band": mate}, device_id_type=MESH)
            greet() if cond is None else pl.when(cond)(greet)
    else:
        @pl.loop(1, n)
        def _(shift):
            pl.semaphore_signal(barrier, inc=1, device_id={"band": lax.rem(me + shift, n)}, device_id_type=MESH)
    for shift in range(1, groups):
        pl.semaphore_signal(barrier, inc=1, device_id={"slab": lax.rem(slab + shift, groups)}, device_id_type=MESH)

    mine = pl.multiple_of(me * frows, 16)
    gathered[pl.ds(mine, beads), :] = feats_ref[...]
    stiff = stiff_ref[...]
    high = stiff.astype(jnp.bfloat16).astype(jnp.float32)
    mid = (stiff - high).astype(jnp.bfloat16).astype(jnp.float32)
    low = stiff - high - mid
    parts = jnp.concatenate([high, mid, low], axis=0)
    tail = jnp.concatenate([parts, jnp.zeros((TAIL - parts.shape[0], parts.shape[1]), jnp.float32)], axis=0)
    gathered[pl.ds(mine + beads, TAIL), :] = tail.astype(jnp.bfloat16)

    if tree:
        inner = jnp.logical_and(z > 0, z < n // 4 - 1)
        pl.semaphore_wait(barrier, jnp.where(inner, groups + 3, groups + 2))
    else:
        pl.semaphore_wait(barrier, n - 1 + groups - 1)

    half = beads // 2
    drain_feats = gather(n, me, gathered, frows, ((0, half), (half, half + TAIL)), fsend, frecv)
    for origin in range(n):
        wide[pl.ds(origin * beads, beads), :] = gathered[pl.ds(origin * frows, beads), :].astype(jnp.float32)

    chunk = 16
    first = pl.multiple_of(me * beads, 16)

    @pl.loop(0, beads // chunk)
    def _(step):
        base = pl.multiple_of(step * chunk, chunk)
        for link in range(links):
            for bead in range(chunk):
                row = nbrs_ref[link * beads + base + bead]
                near[pl.ds(link * chunk + bead, 1), :] = wide[pl.ds(row, 1), :]
        own = feats_ref[pl.ds(base, chunk), :].astype(jnp.float32)
        mixed = near[...].reshape(links, chunk, -1) * own[None]
        mixed = mixed.reshape(links * chunk, -1).astype(jnp.bfloat16)
        pre = jnp.dot(mixed, w_ref[...], preferred_element_type=jnp.float32)
        total = jnp.sum(jnp.tanh(pre).reshape(links, chunk, -1), axis=0)
        slab_ref[pl.ds(first + base, chunk), :] = (total * scale).astype(jnp.bfloat16)

    drain_slab = gather(n, me, slab_ref, beads, ((0, half), (half, half)), ssend, srecv)

    chosen = order_ref[:, 0:1]
    blocks = slab_ref.shape[0] // block
    passed = [(chosen >= (r + 1) * groups).astype(jnp.int32) for r in range(blocks)]
    number = sum(passed)
    lane = chosen - number * groups

    def mask(flag, lanes):
        return jnp.broadcast_to(flag.astype(jnp.float32), (16, lanes)).astype(jnp.bfloat16)

    channels = slab_ref.shape[1]
    masks = [mask(number == r, channels) for r in range(blocks)]
    for row in range(0, block, 16):
        picked = sum(slab_ref[r * block + row:r * block + row + 16, :] * masks[r] for r in range(blocks))
        pivots[pl.ds(pl.multiple_of(slab * block + row, 16), 16), :] = picked

    def pivot_copy(shift, source):
        part = pivots.at[pl.ds(pl.multiple_of(source * block, 16), block), :]
        return pltpu.make_async_remote_copy(
            src_ref=part, dst_ref=part, send_sem=psend.at[shift], recv_sem=precv.at[shift],
            device_id={"slab": lax.rem(slab + shift, groups)}, device_id_type=MESH,
        )

    for shift in range(1, groups):
        pivot_copy(shift, slab).start()

    def column_copy(shift):
        return pltpu.make_async_remote_copy(
            src_ref=column_ref, dst_ref=column_ref, send_sem=csend.at[shift], recv_sem=crecv,
            device_id={"slab": lax.rem(slab + shift, groups)}, device_id_type=MESH,
        )

    @pl.when(slab == owner)
    def _():
        column_ref[...] = slab_ref[pl.ds(pl.multiple_of(home * block, 16), block), :]
        for shift in range(1, groups):
            column_copy(shift).start()
        for shift in range(1, groups):
            column_copy(shift).wait_send()

    @pl.when(slab != owner)
    def _():
        column_copy(1).wait_recv()

    for shift in range(1, groups):
        pivot_copy(shift, lax.rem(slab + groups - shift, groups)).wait_recv()
    masks = [mask(lane == g, channels) for g in range(groups)]
    for row in range(0, block, 16):
        pivot_ref[row:row + 16, :] = sum(
            pivots[g * block + row:g * block + row + 16, :] * masks[g] for g in range(groups)
        )
    held = sum(
        gathered[b * frows + beads:(b + 1) * frows, :].astype(jnp.float32)
        * jnp.broadcast_to((chosen == b).astype(jnp.float32), (TAIL, gathered.shape[1]))
        for b in range(n)
    )
    lanes = block // held.shape[1]
    pstiff_ref[...] = held[0:lanes] + held[lanes:2 * lanes] + held[2 * lanes:3 * lanes]

    for shift in range(1, groups):
        pivot_copy(shift, slab).wait_send()
    drain_feats()
    drain_slab()


def as_row(pieces):
    return jnp.concatenate([pieces[i:i + 1, :] for i in range(pieces.shape[0])], axis=1)


def eliminate(fp_ref, pstiff_ref, work, whitened, log_ref):
    block, width = fp_ref.shape
    step = 32
    fp = fp_ref[...]
    square = lax.dot_general(fp, fp, (((1,), (1,)), ((), ())), preferred_element_type=jnp.float32)
    rows = lax.broadcasted_iota(jnp.int32, (block, block), 0)
    cols = lax.broadcasted_iota(jnp.int32, (block, block), 1)
    work[:, :block] = square + jnp.where(rows == cols, as_row(pstiff_ref[...]), 0.0)
    work[:, block:] = fp.astype(jnp.float32)
    down = lax.broadcasted_iota(jnp.int32, (step, 1), 0)
    eye = (
        lax.broadcasted_iota(jnp.int32, (step, step), 0) == lax.broadcasted_iota(jnp.int32, (step, step), 1)
    ).astype(jnp.float32)
    logs = jnp.zeros((1, 1), jnp.float32)
    for start in range(0, block, step):
        both = jnp.concatenate([work[start:start + step, start:start + step], eye], axis=1)
        for j in range(step - 1):
            lead = both[j:j + 1, :]
            ratio = both[:, j:j + 1] * (1.0 / lead[:, j:j + 1])
            both = both - jnp.where(down > j, ratio, 0.0) * lead
        diag = jnp.sum(both[:, :step] * eye, axis=1, keepdims=True)
        logs = logs + jnp.sum(jnp.log(diag), axis=0, keepdims=True)
        inverse = both[:, step:] * lax.rsqrt(diag)
        done = jnp.dot(inverse, work[start:start + step, :], precision=HI, preferred_element_type=jnp.float32)
        whitened[start:start + step, :] = done[:, block:]
        after = start + step
        if after < block:
            low = after // 128 * 128
            work[low:, low:] = work[low:, low:] - lax.dot_general(
                done[:, low:block], done[:, low:], (((0,), (0,)), ((), ())),
                precision=HI, preferred_element_type=jnp.float32,
            )
    log_ref[...] = jnp.broadcast_to(logs * (1.0 / (STEPS * block)), log_ref.shape)


def finish_kernel(
    groups, order_ref, slab_ref, column_ref, fp_ref, pstiff_ref, stiff_ref,
    out_ref, log_ref, work, whitened, whigh, wlow, pcol,
):
    me = lax.axis_index("band")
    slab = lax.axis_index("slab")
    r = pl.program_id(0)
    pivot = order_ref[0]
    block = fp_ref.shape[0]
    nt = (((1,), (1,)), ((), ()))

    def panel(rows):
        return lax.dot_general(rows, whigh[...], nt, preferred_element_type=jnp.float32) + lax.dot_general(
            rows, wlow[...], nt, preferred_element_type=jnp.float32
        )

    @pl.when(r == 0)
    def _():
        eliminate(fp_ref, pstiff_ref, work, whitened, log_ref)
        w = whitened[...]
        high = w.astype(jnp.bfloat16)
        whigh[...] = high
        wlow[...] = (w - high.astype(jnp.float32)).astype(jnp.bfloat16)
        pcol[...] = jnp.where(me == pivot, 0.0, panel(column_ref[...])).astype(jnp.bfloat16)

    here = r * groups + slab
    rows = slab_ref[...]
    own = jnp.where(here == pivot, 0.0, panel(rows)).astype(jnp.bfloat16)
    value = lax.dot_general(rows, column_ref[...], nt, preferred_element_type=jnp.float32)
    value = value - lax.dot_general(own, pcol[...], nt, preferred_element_type=jnp.float32)
    iota = [lax.broadcasted_iota(jnp.int32, value.shape, d) for d in (0, 1)]
    on = jnp.logical_and(iota[0] == iota[1], here == me)
    value = value + jnp.where(on, as_row(stiff_ref[...]), 0.0)
    parts = block // 128
    for part in range(parts):
        out_ref[pl.ds(part, block, stride=parts), :] = value[:, part * 128:(part + 1) * 128]


def on_device(n, groups, feats, nbrs, w_pair, stiff, order):
    own_feats = feats[0]
    beads, width = own_feats.shape
    links = nbrs.shape[2]
    channels = w_pair.shape[1]
    block = stiff.shape[0]
    count = n * beads
    flat = nbrs[0].T.reshape(links * beads)
    stiff2 = stiff.reshape(block // 128, 128)
    scale = 1.5 / math.sqrt(links * channels)
    vmem = pl.BlockSpec(memory_space=pltpu.VMEM)
    smem = pl.BlockSpec(memory_space=pltpu.SMEM)
    dma = pltpu.SemaphoreType.DMA
    slab_factor, column, pivot_factor, pivot_stiff = pl.pallas_call(
        functools.partial(assemble_kernel, n, groups, block, scale),
        out_shape=(
            jax.ShapeDtypeStruct((count, channels), jnp.bfloat16),
            jax.ShapeDtypeStruct((block, channels), jnp.bfloat16),
            jax.ShapeDtypeStruct((block, channels), jnp.bfloat16),
            jax.ShapeDtypeStruct((block // 128, 128), jnp.float32),
        ),
        in_specs=[vmem, smem, vmem, vmem, vmem],
        out_specs=(vmem, vmem, vmem, vmem),
        scratch_shapes=[
            pltpu.VMEM((n * (beads + TAIL), width), jnp.bfloat16),
            pltpu.VMEM((count, width), jnp.float32),
            pltpu.VMEM((links * 16, width), jnp.float32),
            pltpu.VMEM((groups * block, channels), jnp.bfloat16),
            dma((n * 8,)), dma((n * 2,)), dma((n * 8,)), dma((n * 2,)),
            dma((groups,)), dma(()), dma((groups,)), dma((groups,)),
        ],
        compiler_params=pltpu.CompilerParams(
            collective_id=0, has_side_effects=True, vmem_limit_bytes=32 * 1024 * 1024
        ),
        name="assemble",
    )(order.reshape(1, -1), flat, own_feats, w_pair, stiff2)

    whole = lambda shape: pl.BlockSpec(shape, lambda r: (0,) * len(shape))
    out, logs = pl.pallas_call(
        functools.partial(finish_kernel, groups),
        grid=(count // block,),
        out_shape=(
            jax.ShapeDtypeStruct((count * block // 128, 128), jnp.float32),
            jax.ShapeDtypeStruct((8, 128), jnp.float32),
        ),
        in_specs=[
            smem,
            pl.BlockSpec((block, channels), lambda r: (r, 0)),
            whole((block, channels)), whole((block, channels)),
            whole((block // 128, 128)), whole((block // 128, 128)),
        ],
        out_specs=(
            pl.BlockSpec((block * block // 128, 128), lambda r: (r, 0)),
            whole((8, 128)),
        ),
        scratch_shapes=[
            pltpu.VMEM((block, block + channels), jnp.float32),
            pltpu.VMEM((block, channels), jnp.float32),
            pltpu.VMEM((block, channels), jnp.bfloat16),
            pltpu.VMEM((block, channels), jnp.bfloat16),
            pltpu.VMEM((block, block), jnp.bfloat16),
        ],
        compiler_params=pltpu.CompilerParams(vmem_limit_bytes=32 * 1024 * 1024),
        name="finish",
    )(order, slab_factor, column, pivot_factor, pivot_stiff, stiff2)
    return out.reshape(1, count, 1, block), logs[0, 0]


def solution(mesh):
    in_specs = (P("slab", "band", None), P("slab", "band", None), P(), P("band"), P())
    out_specs = (P("slab", None, "band", None), P())
    return jax.shard_map(
        functools.partial(on_device, mesh.shape["band"], mesh.shape["slab"]),
        mesh=mesh, in_specs=in_specs, out_specs=out_specs, check_vma=False,
    )
```

```python
import functools
import math

import jax
import jax.numpy as jnp
from jax import lax
from jax.experimental import pallas as pl
from jax.experimental.pallas import tpu as pltpu
from jax.sharding import PartitionSpec as P

STEPS = 1
MESH = pl.DeviceIdType.MESH
TAIL = 16
HI = lax.Precision.HIGHEST


def slots(buf, origin, rows, piece):
    start, size = piece
    return buf.at[pl.ds(pl.multiple_of(origin * rows + start, 16), size), :]


def tree_gather(n, me, buf, rows, pieces, send_sem, recv_sem, make=None):
    depth = n // 4
    z, y, x = me // 4, (me // 2) % 2, me % 2
    xn = me + 1 - 2 * x
    yn = me + 2 - 4 * y
    xyn = xn + 2 - 4 * y
    targets = (me + 4, me - 4, xn, yn)
    sent = []

    def copy(origin, piece, way):
        block = slots(buf, origin, rows, pieces[piece])
        return pltpu.make_async_remote_copy(
            src_ref=block,
            dst_ref=block,
            send_sem=send_sem.at[(origin * 2 + piece) * 4 + way],
            recv_sem=recv_sem.at[origin * 2 + piece],
            device_id={"band": targets[way]},
            device_id_type=MESH,
        )

    def send(origin, piece, way, cond):
        sent.append((origin, piece, way, cond))
        if cond is None:
            copy(origin, piece, way).start()
        else:
            pl.when(cond)(lambda: copy(origin, piece, way).start())

    def arrived(origin, piece, cond):
        if cond is None:
            copy(origin, piece, 2).wait_recv()
        else:
            pl.when(cond)(lambda: copy(origin, piece, 2).wait_recv())

    def both(a, b):
        return b if a is None else jnp.logical_and(a, b)

    def exists(dz):
        if dz == 0:
            return None
        return z < depth - dz if dz > 0 else z >= -dz

    def line(dz):
        cond = exists(dz)
        origin = me + 4 * dz
        for piece in (0, 1):
            if dz:
                arrived(origin, piece, cond)
            elif make is not None:
                make(piece)
            if dz <= 0:
                send(origin, piece, 0, both(cond, z < depth - 1))
            if dz >= 0:
                send(origin, piece, 1, both(cond, z > 0))
            for way in (2 + piece, 3 - piece):
                send(origin, piece, way, cond)

    def side(dz):
        cond = exists(dz)
        arrived(xn + 4 * dz, 0, cond)
        send(xn + 4 * dz, 0, 3, cond)
        arrived(yn + 4 * dz, 1, cond)
        send(yn + 4 * dz, 1, 2, cond)

    line(0)
    for far in range(1, depth + 1):
        if far < depth:
            line(far)
            line(-far)
        side(far - 1)
        if far > 1:
            side(1 - far)
    for dz in range(1 - depth, depth):
        cond = exists(dz)
        arrived(yn + 4 * dz, 0, cond)
        arrived(xyn + 4 * dz, 0, cond)
        arrived(xn + 4 * dz, 1, cond)
        arrived(xyn + 4 * dz, 1, cond)

    def drain():
        for origin, piece, way, cond in sent:
            if cond is None:
                copy(origin, piece, way).wait_send()
            else:
                pl.when(cond)(functools.partial(lambda o, p, w: copy(o, p, w).wait_send(), origin, piece, way))

    return drain


def direct_gather(n, me, buf, rows, pieces, send_sem, recv_sem, make=None):
    whole = (0, sum(size for _, size in pieces))

    def copy(origin, shift):
        block = slots(buf, origin, rows, whole)
        return pltpu.make_async_remote_copy(
            src_ref=block,
            dst_ref=block,
            send_sem=send_sem.at[shift],
            recv_sem=recv_sem.at[shift],
            device_id={"band": lax.rem(me + shift, n)},
            device_id_type=MESH,
        )

    if make is not None:
        make(0)
        make(1)

    @pl.loop(1, n)
    def _(shift):
        copy(me, shift).start()

    @pl.loop(1, n)
    def _(shift):
        copy(lax.rem(me + n - shift, n), shift).wait_recv()

    def drain():
        @pl.loop(1, n)
        def _(shift):
            copy(me, shift).wait_send()

    return drain


def assemble_kernel(
    n, groups, block, scale,
    order_ref, nbrs_ref, feats_ref, w_ref, stiff_ref,
    slab_ref, column_ref, pivot_ref, pstiff_ref,
    gathered, wide, near, pivots,
    fsend, frecv, ssend, srecv, csend, crecv, psend, precv,
):
    me = lax.axis_index("band")
    slab = lax.axis_index("slab")
    beads = feats_ref.shape[0]
    links = nbrs_ref.shape[0] // beads
    frows = beads + TAIL
    tree = n == 16
    gather = tree_gather if tree else direct_gather
    home = me // groups
    owner = lax.rem(me, groups)

    barrier = pltpu.get_barrier_semaphore()
    if tree:
        z, y, x = me // 4, (me // 2) % 2, me % 2
        mates = [(me + 1 - 2 * x, None), (me + 2 - 4 * y, None), (me + 4, z < n // 4 - 1), (me - 4, z > 0)]
        for mate, cond in mates:
            def greet(mate=mate):
                pl.semaphore_signal(barrier, inc=1, device_id={"band": mate}, device_id_type=MESH)
            greet() if cond is None else pl.when(cond)(greet)
    else:
        @pl.loop(1, n)
        def _(shift):
            pl.semaphore_signal(barrier, inc=1, device_id={"band": lax.rem(me + shift, n)}, device_id_type=MESH)
    for shift in range(1, groups):
        pl.semaphore_signal(barrier, inc=1, device_id={"slab": lax.rem(slab + shift, groups)}, device_id_type=MESH)

    mine = pl.multiple_of(me * frows, 16)
    gathered[pl.ds(mine, beads), :] = feats_ref[...]
    stiff = stiff_ref[...]
    high = stiff.astype(jnp.bfloat16).astype(jnp.float32)
    mid = (stiff - high).astype(jnp.bfloat16).astype(jnp.float32)
    low = stiff - high - mid
    parts = jnp.concatenate([high, mid, low], axis=0)
    tail = jnp.concatenate([parts, jnp.zeros((TAIL - parts.shape[0], parts.shape[1]), jnp.float32)], axis=0)
    gathered[pl.ds(mine + beads, TAIL), :] = tail.astype(jnp.bfloat16)

    if tree:
        inner = jnp.logical_and(z > 0, z < n // 4 - 1)
        pl.semaphore_wait(barrier, jnp.where(inner, groups + 3, groups + 2))
    else:
        pl.semaphore_wait(barrier, n - 1 + groups - 1)

    half = beads // 2
    drain_feats = gather(n, me, gathered, frows, ((0, half), (half, half + TAIL)), fsend, frecv)
    for origin in range(n):
        wide[pl.ds(origin * beads, beads), :] = gathered[pl.ds(origin * frows, beads), :].astype(jnp.float32)

    chunk = 16
    first = pl.multiple_of(me * beads, 16)

    def make(piece):
        @pl.loop(piece * half // chunk, (piece + 1) * half // chunk)
        def _(step):
            base = pl.multiple_of(step * chunk, chunk)
            for link in range(links):
                for bead in range(chunk):
                    row = nbrs_ref[link * beads + base + bead]
                    near[pl.ds(link * chunk + bead, 1), :] = wide[pl.ds(row, 1), :]
            own = feats_ref[pl.ds(base, chunk), :].astype(jnp.float32)
            mixed = near[...].reshape(links, chunk, -1) * own[None]
            mixed = mixed.reshape(links * chunk, -1).astype(jnp.bfloat16)
            pre = jnp.dot(mixed, w_ref[...], preferred_element_type=jnp.float32)
            total = jnp.sum(jnp.tanh(pre).reshape(links, chunk, -1), axis=0)
            slab_ref[pl.ds(first + base, chunk), :] = (total * scale).astype(jnp.bfloat16)

    drain_slab = gather(n, me, slab_ref, beads, ((0, half), (half, half)), ssend, srecv, make)

    chosen = order_ref[:, 0:1]
    blocks = slab_ref.shape[0] // block
    passed = [(chosen >= (r + 1) * groups).astype(jnp.int32) for r in range(blocks)]
    number = sum(passed)
    lane = chosen - number * groups

    def mask(flag, lanes):
        return jnp.broadcast_to(flag.astype(jnp.float32), (16, lanes)).astype(jnp.bfloat16)

    channels = slab_ref.shape[1]
    masks = [mask(number == r, channels) for r in range(blocks)]
    for row in range(0, block, 16):
        picked = sum(slab_ref[r * block + row:r * block + row + 16, :] * masks[r] for r in range(blocks))
        pivots[pl.ds(pl.multiple_of(slab * block + row, 16), 16), :] = picked

    def pivot_copy(shift, source):
        part = pivots.at[pl.ds(pl.multiple_of(source * block, 16), block), :]
        return pltpu.make_async_remote_copy(
            src_ref=part, dst_ref=part, send_sem=psend.at[shift], recv_sem=precv.at[shift],
            device_id={"slab": lax.rem(slab + shift, groups)}, device_id_type=MESH,
        )

    for shift in range(1, groups):
        pivot_copy(shift, slab).start()

    def column_copy(shift):
        return pltpu.make_async_remote_copy(
            src_ref=column_ref, dst_ref=column_ref, send_sem=csend.at[shift], recv_sem=crecv,
            device_id={"slab": lax.rem(slab + shift, groups)}, device_id_type=MESH,
        )

    @pl.when(slab == owner)
    def _():
        column_ref[...] = slab_ref[pl.ds(pl.multiple_of(home * block, 16), block), :]
        for shift in range(1, groups):
            column_copy(shift).start()
        for shift in range(1, groups):
            column_copy(shift).wait_send()

    @pl.when(slab != owner)
    def _():
        column_copy(1).wait_recv()

    for shift in range(1, groups):
        pivot_copy(shift, lax.rem(slab + groups - shift, groups)).wait_recv()
    masks = [mask(lane == g, channels) for g in range(groups)]
    for row in range(0, block, 16):
        pivot_ref[row:row + 16, :] = sum(
            pivots[g * block + row:g * block + row + 16, :] * masks[g] for g in range(groups)
        )
    held = sum(
        gathered[b * frows + beads:(b + 1) * frows, :].astype(jnp.float32)
        * jnp.broadcast_to((chosen == b).astype(jnp.float32), (TAIL, gathered.shape[1]))
        for b in range(n)
    )
    lanes = block // held.shape[1]
    pstiff_ref[...] = held[0:lanes] + held[lanes:2 * lanes] + held[2 * lanes:3 * lanes]

    for shift in range(1, groups):
        pivot_copy(shift, slab).wait_send()
    drain_feats()
    drain_slab()


def as_row(pieces):
    return jnp.concatenate([pieces[i:i + 1, :] for i in range(pieces.shape[0])], axis=1)


def split(value):
    high = value.astype(jnp.bfloat16)
    return high, (value - high.astype(jnp.float32)).astype(jnp.bfloat16)


def dot3(left, right, dims):
    lh, ll = split(left)
    rh, rl = split(right)
    dims = (dims, ((), ()))
    mul = lambda a, b: lax.dot_general(a, b, dims, preferred_element_type=jnp.float32)
    return mul(lh, rh) + (mul(lh, rl) + mul(ll, rh))


def small_inverse(both):
    size, lanes = both.shape
    kept = []
    for start in range(0, size, 8):
        rows = both.shape[0]
        down = lax.broadcasted_iota(jnp.int32, (rows, lanes), 0)
        cols = [jnp.broadcast_to(both[:, start + m:start + m + 1], (rows, lanes)) for m in range(8)]
        for k in range(8):
            ratio = jnp.where(down > k, cols[k] * (1.0 / cols[k][k:k + 1, :]), 0.0)
            for m in range(k + 1, 8):
                cols[m] = cols[m] - ratio * cols[m][k:k + 1, :]
            both = both - ratio * both[k:k + 1, :]
        kept.append(both[:8])
        both = both[8:]
    return jnp.concatenate(kept, axis=0)


def eliminate(fp_ref, pstiff_ref, work, ident, lowinv, log_ref):
    block = fp_ref.shape[0]
    step = 32
    fp = fp_ref[...]
    square = lax.dot_general(fp, fp, (((1,), (1,)), ((), ())), preferred_element_type=jnp.float32)
    rows = lax.broadcasted_iota(jnp.int32, (block, block), 0)
    cols = lax.broadcasted_iota(jnp.int32, (block, block), 1)
    work[...] = square + jnp.where(rows == cols, as_row(pstiff_ref[...]), 0.0)
    ident[...] = (rows == cols).astype(jnp.float32)
    lowinv[...] = jnp.zeros(lowinv.shape, jnp.float32)
    eye = (
        lax.broadcasted_iota(jnp.int32, (step, step), 0) == lax.broadcasted_iota(jnp.int32, (step, step), 1)
    ).astype(jnp.float32)
    logs = jnp.zeros((1, 1), jnp.float32)
    for start in range(0, block, step):
        after = start + step
        both = small_inverse(jnp.concatenate([work[start:after, start:after], eye], axis=1))
        diag = jnp.sum(both[:, :step] * eye, axis=1, keepdims=True)
        logs = logs + jnp.sum(jnp.log(diag), axis=0, keepdims=True)
        inverse = both[:, step:] * lax.rsqrt(diag)
        low = after // 128 * 128
        high = -(-after // 128) * 128
        if after == block:
            lowinv[start:after, :] = dot3(inverse, ident[start:after, :], ((1,), (0,)))
            break
        wide = jnp.concatenate([work[start:after, low:], ident[start:after, :high]], axis=1)
        done = dot3(inverse, wide, ((1,), (0,)))
        lowinv[start:after, :high] = done[:, block - low:]
        change = dot3(done[:, :block - low], done, ((0,), (0,)))
        work[low:, low:] = work[low:, low:] - change[:, :block - low]
        ident[low:, :high] = ident[low:, :high] - change[:, block - low:]
    log_ref[...] = jnp.broadcast_to(logs * (1.0 / (STEPS * block)), log_ref.shape)


def finish_kernel(
    groups, order_ref, slab_ref, column_ref, fp_ref, pstiff_ref, stiff_ref,
    out_ref, log_ref, work, ident, lowinv, whigh, wlow, pcol,
):
    me = lax.axis_index("band")
    slab = lax.axis_index("slab")
    r = pl.program_id(0)
    pivot = order_ref[0]
    block = fp_ref.shape[0]
    nt = (((1,), (1,)), ((), ()))

    def panel(rows):
        return lax.dot_general(rows, whigh[...], nt, preferred_element_type=jnp.float32) + lax.dot_general(
            rows, wlow[...], nt, preferred_element_type=jnp.float32
        )

    @pl.when(r == 0)
    def _():
        eliminate(fp_ref, pstiff_ref, work, ident, lowinv, log_ref)
        ih, il = split(lowinv[...])
        fp = fp_ref[...]
        w = jnp.dot(ih, fp, preferred_element_type=jnp.float32) + jnp.dot(
            il, fp, preferred_element_type=jnp.float32
        )
        whigh[...], wlow[...] = split(w)
        pcol[...] = jnp.where(me == pivot, 0.0, panel(column_ref[...])).astype(jnp.bfloat16)

    here = r * groups + slab
    rows = slab_ref[...]
    own = jnp.where(here == pivot, 0.0, panel(rows)).astype(jnp.bfloat16)
    value = lax.dot_general(rows, column_ref[...], nt, preferred_element_type=jnp.float32)
    value = value - lax.dot_general(own, pcol[...], nt, preferred_element_type=jnp.float32)
    iota = [lax.broadcasted_iota(jnp.int32, value.shape, d) for d in (0, 1)]
    on = jnp.logical_and(iota[0] == iota[1], here == me)
    value = value + jnp.where(on, as_row(stiff_ref[...]), 0.0)
    parts = block // 128
    for part in range(parts):
        out_ref[pl.ds(part, block, stride=parts), :] = value[:, part * 128:(part + 1) * 128]


def on_device(n, groups, feats, nbrs, w_pair, stiff, order):
    own_feats = feats[0]
    beads, width = own_feats.shape
    links = nbrs.shape[2]
    channels = w_pair.shape[1]
    block = stiff.shape[0]
    count = n * beads
    flat = nbrs[0].T.reshape(links * beads)
    stiff2 = stiff.reshape(block // 128, 128)
    scale = 1.5 / math.sqrt(links * channels)
    vmem = pl.BlockSpec(memory_space=pltpu.VMEM)
    smem = pl.BlockSpec(memory_space=pltpu.SMEM)
    dma = pltpu.SemaphoreType.DMA
    slab_factor, column, pivot_factor, pivot_stiff = pl.pallas_call(
        functools.partial(assemble_kernel, n, groups, block, scale),
        out_shape=(
            jax.ShapeDtypeStruct((count, channels), jnp.bfloat16),
            jax.ShapeDtypeStruct((block, channels), jnp.bfloat16),
            jax.ShapeDtypeStruct((block, channels), jnp.bfloat16),
            jax.ShapeDtypeStruct((block // 128, 128), jnp.float32),
        ),
        in_specs=[vmem, smem, vmem, vmem, vmem],
        out_specs=(vmem, vmem, vmem, vmem),
        scratch_shapes=[
            pltpu.VMEM((n * (beads + TAIL), width), jnp.bfloat16),
            pltpu.VMEM((count, width), jnp.float32),
            pltpu.VMEM((links * 16, width), jnp.float32),
            pltpu.VMEM((groups * block, channels), jnp.bfloat16),
            dma((n * 8,)), dma((n * 2,)), dma((n * 8,)), dma((n * 2,)),
            dma((groups,)), dma(()), dma((groups,)), dma((groups,)),
        ],
        compiler_params=pltpu.CompilerParams(
            collective_id=0, has_side_effects=True, vmem_limit_bytes=32 * 1024 * 1024
        ),
        name="assemble",
    )(order.reshape(1, -1), flat, own_feats, w_pair, stiff2)

    whole = lambda shape: pl.BlockSpec(shape, lambda r: (0,) * len(shape))
    out, logs = pl.pallas_call(
        functools.partial(finish_kernel, groups),
        grid=(count // block,),
        out_shape=(
            jax.ShapeDtypeStruct((count * block // 128, 128), jnp.float32),
            jax.ShapeDtypeStruct((8, 128), jnp.float32),
        ),
        in_specs=[
            smem,
            pl.BlockSpec((block, channels), lambda r: (r, 0)),
            whole((block, channels)), whole((block, channels)),
            whole((block // 128, 128)), whole((block // 128, 128)),
        ],
        out_specs=(
            pl.BlockSpec((block * block // 128, 128), lambda r: (r, 0)),
            whole((8, 128)),
        ),
        scratch_shapes=[
            pltpu.VMEM((block, block), jnp.float32),
            pltpu.VMEM((block, block), jnp.float32),
            pltpu.VMEM((block, block), jnp.float32),
            pltpu.VMEM((block, channels), jnp.bfloat16),
            pltpu.VMEM((block, channels), jnp.bfloat16),
            pltpu.VMEM((block, block), jnp.bfloat16),
        ],
        compiler_params=pltpu.CompilerParams(vmem_limit_bytes=32 * 1024 * 1024),
        name="finish",
    )(order, slab_factor, column, pivot_factor, pivot_stiff, stiff2)
    return out.reshape(1, count, 1, block), logs[0, 0]


def solution(mesh):
    in_specs = (P("slab", "band", None), P("slab", "band", None), P(), P("band"), P())
    out_specs = (P("slab", None, "band", None), P())
    return jax.shard_map(
        functools.partial(on_device, mesh.shape["band"], mesh.shape["slab"]),
        mesh=mesh, in_specs=in_specs, out_specs=out_specs, check_vma=False,
    )
```

```python
import functools
import math

import jax
import jax.numpy as jnp
from jax import lax
from jax.experimental import pallas as pl
from jax.experimental.pallas import tpu as pltpu
from jax.sharding import PartitionSpec as P

STEPS = 1
MESH = pl.DeviceIdType.MESH
TAIL = 16
HI = lax.Precision.HIGHEST


def slots(buf, origin, rows, piece):
    start, size = piece
    return buf.at[pl.ds(pl.multiple_of(origin * rows + start, 16), size), :]


def tree_gather(n, me, buf, rows, pieces, send_sem, recv_sem, make=None):
    depth = n // 4
    z, y, x = me // 4, (me // 2) % 2, me % 2
    xn = me + 1 - 2 * x
    yn = me + 2 - 4 * y
    xyn = xn + 2 - 4 * y
    targets = (me + 4, me - 4, xn, yn)
    sent = []

    def copy(origin, piece, way):
        block = slots(buf, origin, rows, pieces[piece])
        return pltpu.make_async_remote_copy(
            src_ref=block,
            dst_ref=block,
            send_sem=send_sem.at[(origin * 2 + piece) * 4 + way],
            recv_sem=recv_sem.at[origin * 2 + piece],
            device_id={"band": targets[way]},
            device_id_type=MESH,
        )

    def send(origin, piece, way, cond):
        sent.append((origin, piece, way, cond))
        if cond is None:
            copy(origin, piece, way).start()
        else:
            pl.when(cond)(lambda: copy(origin, piece, way).start())

    def arrived(origin, piece, cond):
        if cond is None:
            copy(origin, piece, 2).wait_recv()
        else:
            pl.when(cond)(lambda: copy(origin, piece, 2).wait_recv())

    def both(a, b):
        return b if a is None else jnp.logical_and(a, b)

    def exists(dz):
        if dz == 0:
            return None
        return z < depth - dz if dz > 0 else z >= -dz

    def line(dz):
        cond = exists(dz)
        origin = me + 4 * dz
        for piece in (0, 1):
            if dz:
                arrived(origin, piece, cond)
            elif make is not None:
                make(piece)
            if dz <= 0:
                send(origin, piece, 0, both(cond, z < depth - 1))
            if dz >= 0:
                send(origin, piece, 1, both(cond, z > 0))
            for way in (2 + piece, 3 - piece):
                send(origin, piece, way, cond)

    def side(dz):
        cond = exists(dz)
        arrived(xn + 4 * dz, 0, cond)
        send(xn + 4 * dz, 0, 3, cond)
        arrived(yn + 4 * dz, 1, cond)
        send(yn + 4 * dz, 1, 2, cond)

    line(0)
    for far in range(1, depth + 1):
        if far < depth:
            line(far)
            line(-far)
        side(far - 1)
        if far > 1:
            side(1 - far)
    for dz in range(1 - depth, depth):
        cond = exists(dz)
        arrived(yn + 4 * dz, 0, cond)
        arrived(xyn + 4 * dz, 0, cond)
        arrived(xn + 4 * dz, 1, cond)
        arrived(xyn + 4 * dz, 1, cond)

    def drain():
        for origin, piece, way, cond in sent:
            if cond is None:
                copy(origin, piece, way).wait_send()
            else:
                pl.when(cond)(functools.partial(lambda o, p, w: copy(o, p, w).wait_send(), origin, piece, way))

    return drain


def short_gather(n, me, buf, rows, pieces, send_sem, recv_sem):
    depth = n // 4
    z, y, x = me // 4, (me // 2) % 2, me % 2
    xn = me + 1 - 2 * x
    yn = me + 2 - 4 * y
    corners = (xn, yn, xn + 2 - 4 * y)
    whole = (0, sum(size for _, size in pieces))

    def line(base, turn):
        return base % 4 + lax.rem(z + turn, depth) * 4

    def copy(origin, sem, target):
        block = slots(buf, origin, rows, whole)
        return pltpu.make_async_remote_copy(
            src_ref=block,
            dst_ref=block,
            send_sem=send_sem.at[sem],
            recv_sem=recv_sem.at[origin],
            device_id={"band": target},
            device_id_type=MESH,
        )

    sent = []

    def send(origin, target):
        item = copy(origin, len(sent), target)
        item.start()
        sent.append(item)

    for turn in range(1, depth):
        send(me, line(me, turn))
    for corner in corners:
        send(me, corner)
    for turn in range(1, depth):
        origin = line(me, depth - turn)
        copy(origin, 0, me).wait_recv()
        for corner in corners:
            send(origin, corner)
    for turn in range(depth):
        for corner in corners:
            copy(line(corner, turn), 0, me).wait_recv()

    def drain():
        for item in sent:
            item.wait_send()

    return drain


def direct_gather(n, me, buf, rows, pieces, send_sem, recv_sem, make=None):
    whole = (0, sum(size for _, size in pieces))

    def copy(origin, shift):
        block = slots(buf, origin, rows, whole)
        return pltpu.make_async_remote_copy(
            src_ref=block,
            dst_ref=block,
            send_sem=send_sem.at[shift],
            recv_sem=recv_sem.at[shift],
            device_id={"band": lax.rem(me + shift, n)},
            device_id_type=MESH,
        )

    if make is not None:
        make(0)
        make(1)

    @pl.loop(1, n)
    def _(shift):
        copy(me, shift).start()

    @pl.loop(1, n)
    def _(shift):
        copy(lax.rem(me + n - shift, n), shift).wait_recv()

    def drain():
        @pl.loop(1, n)
        def _(shift):
            copy(me, shift).wait_send()

    return drain


def assemble_kernel(
    n, groups, block, scale,
    order_hbm, nbrs_hbm, feats_hbm, w_hbm, stiff_hbm,
    slab_ref, column_ref, pivot_ref, pstiff_ref, stiff_ref, chosen_ref,
    order_ref, nbrs_ref, w_ref, load_sem, gathered, wide, near, pivots,
    fsend, frecv, ssend, srecv, csend, crecv, psend, precv,
):
    me = lax.axis_index("band")
    slab = lax.axis_index("slab")
    beads = feats_hbm.shape[0]
    links = nbrs_hbm.shape[0] // beads
    frows = beads + TAIL
    tree = n == 16
    gather = tree_gather if tree else direct_gather
    home = me // groups
    owner = lax.rem(me, groups)

    barrier = pltpu.get_barrier_semaphore()
    if tree:
        y, x = (me // 2) % 2, me % 2
        xn, yn = me + 1 - 2 * x, me + 2 - 4 * y
        mates = [xn, yn, xn + 2 - 4 * y] + [lax.rem(me + 4 * turn, n) for turn in range(1, n // 4)]
        for mate in mates:
            pl.semaphore_signal(barrier, inc=1, device_id={"band": mate}, device_id_type=MESH)
    else:
        @pl.loop(1, n)
        def _(shift):
            pl.semaphore_signal(barrier, inc=1, device_id={"band": lax.rem(me + shift, n)}, device_id_type=MESH)
    for shift in range(1, groups):
        pl.semaphore_signal(barrier, inc=1, device_id={"slab": lax.rem(slab + shift, groups)}, device_id_type=MESH)

    mine = pl.multiple_of(me * frows, 16)
    loads = [
        pltpu.make_async_copy(source, target, load_sem.at[i])
        for i, (source, target) in enumerate((
            (stiff_hbm, stiff_ref),
            (feats_hbm, gathered.at[pl.ds(mine, beads), :]),
            (nbrs_hbm, nbrs_ref),
            (w_hbm, w_ref),
            (order_hbm, order_ref),
        ))
    ]
    for load in loads:
        load.start()
    loads[0].wait()
    stiff = stiff_ref[...]
    high = stiff.astype(jnp.bfloat16).astype(jnp.float32)
    mid = (stiff - high).astype(jnp.bfloat16).astype(jnp.float32)
    low = stiff - high - mid
    parts = jnp.concatenate([high, mid, low], axis=0)
    tail = jnp.concatenate([parts, jnp.zeros((TAIL - parts.shape[0], parts.shape[1]), jnp.float32)], axis=0)
    gathered[pl.ds(mine + beads, TAIL), :] = tail.astype(jnp.bfloat16)
    loads[1].wait()

    if tree:
        pl.semaphore_wait(barrier, len(mates) + groups - 1)
    else:
        pl.semaphore_wait(barrier, n - 1 + groups - 1)

    half = beads // 2
    drain_feats = (short_gather if tree else direct_gather)(n, me, gathered, frows, ((0, half), (half, half + TAIL)), fsend, frecv)
    for load in loads[2:]:
        load.wait()
    for origin in range(n):
        wide[pl.ds(origin * beads, beads), :] = gathered[pl.ds(origin * frows, beads), :].astype(jnp.float32)

    chunk = 16
    first = pl.multiple_of(me * beads, 16)

    def make(piece):
        @pl.loop(piece * half // chunk, (piece + 1) * half // chunk)
        def _(step):
            base = pl.multiple_of(step * chunk, chunk)
            for link in range(links):
                for bead in range(chunk):
                    row = nbrs_ref[link * beads + base + bead]
                    near[pl.ds(link * chunk + bead, 1), :] = wide[pl.ds(row, 1), :]
            own = gathered[pl.ds(pl.multiple_of(mine + base, 16), chunk), :].astype(jnp.float32)
            mixed = near[...].reshape(links, chunk, -1) * own[None]
            mixed = mixed.reshape(links * chunk, -1).astype(jnp.bfloat16)
            pre = jnp.dot(mixed, w_ref[...], preferred_element_type=jnp.float32)
            total = jnp.sum(jnp.tanh(pre).reshape(links, chunk, -1), axis=0)
            slab_ref[pl.ds(first + base, chunk), :] = (total * scale).astype(jnp.bfloat16)

    drain_slab = gather(n, me, slab_ref, beads, ((0, half), (half, half)), ssend, srecv, make)

    chosen = order_ref[:, 0:1]
    chosen_ref[...] = jnp.broadcast_to(chosen, chosen_ref.shape)
    blocks = slab_ref.shape[0] // block
    passed = [(chosen >= (r + 1) * groups).astype(jnp.int32) for r in range(blocks)]
    number = sum(passed)
    lane = chosen - number * groups

    def mask(flag, lanes):
        return jnp.broadcast_to(flag.astype(jnp.float32), (16, lanes)).astype(jnp.bfloat16)

    channels = slab_ref.shape[1]
    masks = [mask(number == r, channels) for r in range(blocks)]
    for row in range(0, block, 16):
        picked = sum(slab_ref[r * block + row:r * block + row + 16, :] * masks[r] for r in range(blocks))
        pivots[pl.ds(pl.multiple_of(slab * block + row, 16), 16), :] = picked

    def pivot_copy(shift, source):
        part = pivots.at[pl.ds(pl.multiple_of(source * block, 16), block), :]
        return pltpu.make_async_remote_copy(
            src_ref=part, dst_ref=part, send_sem=psend.at[shift], recv_sem=precv.at[shift],
            device_id={"slab": lax.rem(slab + shift, groups)}, device_id_type=MESH,
        )

    for shift in range(1, groups):
        pivot_copy(shift, slab).start()

    def column_copy(shift):
        return pltpu.make_async_remote_copy(
            src_ref=column_ref, dst_ref=column_ref, send_sem=csend.at[shift], recv_sem=crecv,
            device_id={"slab": lax.rem(slab + shift, groups)}, device_id_type=MESH,
        )

    @pl.when(slab == owner)
    def _():
        column_ref[...] = slab_ref[pl.ds(pl.multiple_of(home * block, 16), block), :]
        for shift in range(1, groups):
            column_copy(shift).start()
        for shift in range(1, groups):
            column_copy(shift).wait_send()

    @pl.when(slab != owner)
    def _():
        column_copy(1).wait_recv()

    for shift in range(1, groups):
        pivot_copy(shift, lax.rem(slab + groups - shift, groups)).wait_recv()
    masks = [mask(lane == g, channels) for g in range(groups)]
    for row in range(0, block, 16):
        pivot_ref[row:row + 16, :] = sum(
            pivots[g * block + row:g * block + row + 16, :] * masks[g] for g in range(groups)
        )
    held = sum(
        gathered[b * frows + beads:(b + 1) * frows, :].astype(jnp.float32)
        * jnp.broadcast_to((chosen == b).astype(jnp.float32), (TAIL, gathered.shape[1]))
        for b in range(n)
    )
    lanes = block // held.shape[1]
    pstiff_ref[...] = held[0:lanes] + held[lanes:2 * lanes] + held[2 * lanes:3 * lanes]

    for shift in range(1, groups):
        pivot_copy(shift, slab).wait_send()
    drain_feats()
    drain_slab()


def as_row(pieces):
    return jnp.concatenate([pieces[i:i + 1, :] for i in range(pieces.shape[0])], axis=1)


def split(value):
    high = value.astype(jnp.bfloat16)
    return high, (value - high.astype(jnp.float32)).astype(jnp.bfloat16)


def dot3(left, right, dims):
    lh, ll = split(left)
    rh, rl = split(right)
    dims = (dims, ((), ()))
    mul = lambda a, b: lax.dot_general(a, b, dims, preferred_element_type=jnp.float32)
    return mul(lh, rh) + (mul(lh, rl) + mul(ll, rh))


def small_inverse(both):
    size, lanes = both.shape
    kept = []
    for start in range(0, size, 8):
        rows = both.shape[0]
        down = lax.broadcasted_iota(jnp.int32, (rows, lanes), 0)
        cols = [jnp.broadcast_to(both[:, start + m:start + m + 1], (rows, lanes)) for m in range(8)]
        for k in range(8):
            ratio = jnp.where(down > k, cols[k] * (1.0 / cols[k][k:k + 1, :]), 0.0)
            for m in range(k + 1, 8):
                cols[m] = cols[m] - ratio * cols[m][k:k + 1, :]
            both = both - ratio * both[k:k + 1, :]
        kept.append(both[:8])
        both = both[8:]
    return jnp.concatenate(kept, axis=0)


def eliminate(fp_ref, pstiff_ref, work, ident, lowinv, log_ref):
    block = fp_ref.shape[0]
    step = 32
    fp = fp_ref[...]
    square = lax.dot_general(fp, fp, (((1,), (1,)), ((), ())), preferred_element_type=jnp.float32)
    rows = lax.broadcasted_iota(jnp.int32, (block, block), 0)
    cols = lax.broadcasted_iota(jnp.int32, (block, block), 1)
    work[...] = square + jnp.where(rows == cols, as_row(pstiff_ref[...]), 0.0)
    ident[...] = (rows == cols).astype(jnp.float32)
    lowinv[...] = jnp.zeros(lowinv.shape, jnp.float32)
    eye = (
        lax.broadcasted_iota(jnp.int32, (step, step), 0) == lax.broadcasted_iota(jnp.int32, (step, step), 1)
    ).astype(jnp.float32)
    logs = jnp.zeros((1, 1), jnp.float32)
    for start in range(0, block, step):
        after = start + step
        both = small_inverse(jnp.concatenate([work[start:after, start:after], eye], axis=1))
        diag = jnp.sum(both[:, :step] * eye, axis=1, keepdims=True)
        logs = logs + jnp.sum(jnp.log(diag), axis=0, keepdims=True)
        inverse = both[:, step:] * lax.rsqrt(diag)
        low = after // 128 * 128
        high = -(-after // 128) * 128
        if after == block:
            lowinv[start:after, :] = dot3(inverse, ident[start:after, :], ((1,), (0,)))
            break
        wide = jnp.concatenate([work[start:after, low:], ident[start:after, :high]], axis=1)
        done = dot3(inverse, wide, ((1,), (0,)))
        lowinv[start:after, :high] = done[:, block - low:]
        change = dot3(done[:, :block - low], done, ((0,), (0,)))
        work[low:, low:] = work[low:, low:] - change[:, :block - low]
        ident[low:, :high] = ident[low:, :high] - change[:, block - low:]
    log_ref[0, 0] = jnp.sum(logs) * (1.0 / (STEPS * block))


def finish_kernel(
    groups, chosen_ref, slab_ref, column_ref, fp_ref, pstiff_ref, stiff_ref,
    out_ref, log_ref, work, ident, lowinv, whigh, wlow, pcol,
):
    me = lax.axis_index("band")
    slab = lax.axis_index("slab")
    r = pl.program_id(0)
    pivot = chosen_ref[...]
    block = fp_ref.shape[0]
    nt = (((1,), (1,)), ((), ()))

    def panel(rows):
        return lax.dot_general(rows, whigh[...], nt, preferred_element_type=jnp.float32) + lax.dot_general(
            rows, wlow[...], nt, preferred_element_type=jnp.float32
        )

    @pl.when(r == 0)
    def _():
        eliminate(fp_ref, pstiff_ref, work, ident, lowinv, log_ref)
        ih, il = split(lowinv[...])
        fp = fp_ref[...]
        w = jnp.dot(ih, fp, preferred_element_type=jnp.float32) + jnp.dot(
            il, fp, preferred_element_type=jnp.float32
        )
        whigh[...], wlow[...] = split(w)
        pcol[...] = jnp.where(me == pivot, 0.0, panel(column_ref[...])).astype(jnp.bfloat16)

    here = r * groups + slab
    rows = slab_ref[...]
    own = jnp.where(here == pivot, 0.0, panel(rows)).astype(jnp.bfloat16)
    value = lax.dot_general(rows, column_ref[...], nt, preferred_element_type=jnp.float32)
    value = value - lax.dot_general(own, pcol[...], nt, preferred_element_type=jnp.float32)
    iota = [lax.broadcasted_iota(jnp.int32, value.shape, d) for d in (0, 1)]
    on = jnp.logical_and(iota[0] == iota[1], here == me)
    value = value + jnp.where(on, as_row(stiff_ref[...]), 0.0)
    parts = block // 128
    for part in range(parts):
        out_ref[pl.ds(part, block, stride=parts), :] = value[:, part * 128:(part + 1) * 128]


def on_device(n, groups, feats, nbrs, w_pair, stiff, order):
    own_feats = feats[0]
    beads, width = own_feats.shape
    links = nbrs.shape[2]
    channels = w_pair.shape[1]
    block = stiff.shape[0]
    count = n * beads
    flat = nbrs[0].T.reshape(links * beads)
    stiff2 = stiff.reshape(block // 128, 128)
    scale = 1.5 / math.sqrt(links * channels)
    vmem = pl.BlockSpec(memory_space=pltpu.VMEM)
    hbm = pl.BlockSpec(memory_space=pltpu.HBM)
    dma = pltpu.SemaphoreType.DMA
    slab_factor, column, pivot_factor, pivot_stiff, own_stiff, chosen = pl.pallas_call(
        functools.partial(assemble_kernel, n, groups, block, scale),
        out_shape=(
            jax.ShapeDtypeStruct((count, channels), jnp.bfloat16),
            jax.ShapeDtypeStruct((block, channels), jnp.bfloat16),
            jax.ShapeDtypeStruct((block, channels), jnp.bfloat16),
            jax.ShapeDtypeStruct((block // 128, 128), jnp.float32),
            jax.ShapeDtypeStruct((block // 128, 128), jnp.float32),
            jax.ShapeDtypeStruct((1, block), jnp.int32),
        ),
        in_specs=[hbm] * 5,
        out_specs=(vmem,) * 6,
        scratch_shapes=[
            pltpu.VMEM((1, order.shape[0]), jnp.int32),
            pltpu.SMEM((links * beads,), jnp.int32),
            pltpu.VMEM((width, channels), jnp.bfloat16),
            dma((5,)),
            pltpu.VMEM((n * (beads + TAIL), width), jnp.bfloat16),
            pltpu.VMEM((count, width), jnp.float32),
            pltpu.VMEM((links * 16, width), jnp.float32),
            pltpu.VMEM((groups * block, channels), jnp.bfloat16),
            dma((n * 8,)), dma((n * 2,)), dma((n * 8,)), dma((n * 2,)),
            dma((groups,)), dma(()), dma((groups,)), dma((groups,)),
        ],
        compiler_params=pltpu.CompilerParams(
            collective_id=0, has_side_effects=True, vmem_limit_bytes=60 * 1024 * 1024
        ),
        name="assemble",
    )(order.reshape(1, -1), flat, own_feats, w_pair, stiff2)

    whole = lambda shape: pl.BlockSpec(shape, lambda r: (0,) * len(shape))
    out, logs = pl.pallas_call(
        functools.partial(finish_kernel, groups),
        grid=(count // block,),
        out_shape=(
            jax.ShapeDtypeStruct((count * block // 128, 128), jnp.float32),
            jax.ShapeDtypeStruct((1, 1), jnp.float32),
        ),
        in_specs=[
            whole((1, block)),
            pl.BlockSpec((block, channels), lambda r: (r, 0)),
            whole((block, channels)), whole((block, channels)),
            whole((block // 128, 128)), whole((block // 128, 128)),
        ],
        out_specs=(
            pl.BlockSpec((block * block // 128, 128), lambda r: (r, 0)),
            pl.BlockSpec(memory_space=pltpu.SMEM),
        ),
        scratch_shapes=[
            pltpu.VMEM((block, block), jnp.float32),
            pltpu.VMEM((block, block), jnp.float32),
            pltpu.VMEM((block, block), jnp.float32),
            pltpu.VMEM((block, channels), jnp.bfloat16),
            pltpu.VMEM((block, channels), jnp.bfloat16),
            pltpu.VMEM((block, block), jnp.bfloat16),
        ],
        compiler_params=pltpu.CompilerParams(vmem_limit_bytes=60 * 1024 * 1024),
        name="finish",
    )(chosen, slab_factor, column, pivot_factor, pivot_stiff, own_stiff)
    return out.reshape(1, count, 1, block), logs[0, 0]


def solution(mesh):
    in_specs = (P("slab", "band", None), P("slab", "band", None), P(), P("band"), P())
    out_specs = (P("slab", None, "band", None), P())
    return jax.shard_map(
        functools.partial(on_device, mesh.shape["band"], mesh.shape["slab"]),
        mesh=mesh, in_specs=in_specs, out_specs=out_specs, check_vma=False,
    )
```

```python
import functools
import math

import jax
import jax.numpy as jnp
from jax import lax
from jax.experimental import pallas as pl
from jax.experimental.pallas import tpu as pltpu
from jax.sharding import PartitionSpec as P

STEPS = 1
MESH = pl.DeviceIdType.MESH
TAIL = 16
HI = lax.Precision.HIGHEST


def slots(buf, origin, rows, piece):
    start, size = piece
    return buf.at[pl.ds(pl.multiple_of(origin * rows + start, 16), size), :]


def tree_gather(n, me, buf, rows, pieces, send_sem, recv_sem, make=None):
    depth = n // 4
    z, y, x = me // 4, (me // 2) % 2, me % 2
    xn = me + 1 - 2 * x
    yn = me + 2 - 4 * y
    xyn = xn + 2 - 4 * y
    targets = (me + 4, me - 4, xn, yn)
    sent = []

    def copy(origin, piece, way):
        block = slots(buf, origin, rows, pieces[piece])
        return pltpu.make_async_remote_copy(
            src_ref=block,
            dst_ref=block,
            send_sem=send_sem.at[(origin * 2 + piece) * 4 + way],
            recv_sem=recv_sem.at[origin * 2 + piece],
            device_id={"band": targets[way]},
            device_id_type=MESH,
        )

    def send(origin, piece, way, cond):
        sent.append((origin, piece, way, cond))
        if cond is None:
            copy(origin, piece, way).start()
        else:
            pl.when(cond)(lambda: copy(origin, piece, way).start())

    def arrived(origin, piece, cond):
        if cond is None:
            copy(origin, piece, 2).wait_recv()
        else:
            pl.when(cond)(lambda: copy(origin, piece, 2).wait_recv())

    def both(a, b):
        return b if a is None else jnp.logical_and(a, b)

    def exists(dz):
        if dz == 0:
            return None
        return z < depth - dz if dz > 0 else z >= -dz

    def line(dz):
        cond = exists(dz)
        origin = me + 4 * dz
        for piece in (0, 1):
            if dz:
                arrived(origin, piece, cond)
            elif make is not None:
                make(piece)
            if dz <= 0:
                send(origin, piece, 0, both(cond, z < depth - 1))
            if dz >= 0:
                send(origin, piece, 1, both(cond, z > 0))
            for way in (2 + piece, 3 - piece):
                send(origin, piece, way, cond)

    def side(dz):
        cond = exists(dz)
        arrived(xn + 4 * dz, 0, cond)
        send(xn + 4 * dz, 0, 3, cond)
        arrived(yn + 4 * dz, 1, cond)
        send(yn + 4 * dz, 1, 2, cond)

    line(0)
    for far in range(1, depth + 1):
        if far < depth:
            line(far)
            line(-far)
        side(far - 1)
        if far > 1:
            side(1 - far)
    for dz in range(1 - depth, depth):
        cond = exists(dz)
        arrived(yn + 4 * dz, 0, cond)
        arrived(xyn + 4 * dz, 0, cond)
        arrived(xn + 4 * dz, 1, cond)
        arrived(xyn + 4 * dz, 1, cond)

    def drain():
        for origin, piece, way, cond in sent:
            if cond is None:
                copy(origin, piece, way).wait_send()
            else:
                pl.when(cond)(functools.partial(lambda o, p, w: copy(o, p, w).wait_send(), origin, piece, way))

    return drain


def short_gather(n, me, buf, rows, pieces, send_sem, recv_sem):
    depth = n // 4
    z, y, x = me // 4, (me // 2) % 2, me % 2
    xn = me + 1 - 2 * x
    yn = me + 2 - 4 * y
    corners = (xn, yn, xn + 2 - 4 * y)
    whole = (0, sum(size for _, size in pieces))

    def line(base, turn):
        return base % 4 + lax.rem(z + turn, depth) * 4

    def copy(origin, sem, target):
        block = slots(buf, origin, rows, whole)
        return pltpu.make_async_remote_copy(
            src_ref=block,
            dst_ref=block,
            send_sem=send_sem.at[sem],
            recv_sem=recv_sem.at[origin],
            device_id={"band": target},
            device_id_type=MESH,
        )

    sent = []

    def send(origin, target):
        item = copy(origin, len(sent), target)
        item.start()
        sent.append(item)

    for turn in range(1, depth):
        send(me, line(me, turn))
    for corner in corners:
        send(me, corner)
    for turn in range(1, depth):
        origin = line(me, depth - turn)
        copy(origin, 0, me).wait_recv()
        for corner in corners:
            send(origin, corner)
    for turn in range(depth):
        for corner in corners:
            copy(line(corner, turn), 0, me).wait_recv()

    def drain():
        for item in sent:
            item.wait_send()

    return drain


def direct_gather(n, me, buf, rows, pieces, send_sem, recv_sem, make=None):
    whole = (0, sum(size for _, size in pieces))

    def copy(origin, shift):
        block = slots(buf, origin, rows, whole)
        return pltpu.make_async_remote_copy(
            src_ref=block,
            dst_ref=block,
            send_sem=send_sem.at[shift],
            recv_sem=recv_sem.at[shift],
            device_id={"band": lax.rem(me + shift, n)},
            device_id_type=MESH,
        )

    if make is not None:
        make(0)
        make(1)

    @pl.loop(1, n)
    def _(shift):
        copy(me, shift).start()

    @pl.loop(1, n)
    def _(shift):
        copy(lax.rem(me + n - shift, n), shift).wait_recv()

    def drain():
        @pl.loop(1, n)
        def _(shift):
            copy(me, shift).wait_send()

    return drain


def assemble_kernel(
    n, groups, block, scale,
    order_hbm, nbrs_hbm, feats_hbm, w_hbm, stiff_hbm,
    slab_ref, column_ref, pivot_ref, pstiff_ref, stiff_ref, chosen_ref,
    order_ref, nbrs_ref, w_ref, load_sem, gathered, wide, near, pivots,
    fsend, frecv, ssend, srecv, csend, crecv, psend, precv,
):
    me = lax.axis_index("band")
    slab = lax.axis_index("slab")
    beads = feats_hbm.shape[0]
    links = nbrs_hbm.shape[0] // beads
    frows = beads + TAIL
    tree = n == 16
    gather = tree_gather if tree else direct_gather
    home = me // groups
    owner = lax.rem(me, groups)

    barrier = pltpu.get_barrier_semaphore()
    if tree:
        y, x = (me // 2) % 2, me % 2
        xn, yn = me + 1 - 2 * x, me + 2 - 4 * y
        mates = [xn, yn, xn + 2 - 4 * y] + [lax.rem(me + 4 * turn, n) for turn in range(1, n // 4)]
        for mate in mates:
            pl.semaphore_signal(barrier, inc=1, device_id={"band": mate}, device_id_type=MESH)
    else:
        @pl.loop(1, n)
        def _(shift):
            pl.semaphore_signal(barrier, inc=1, device_id={"band": lax.rem(me + shift, n)}, device_id_type=MESH)
    for shift in range(1, groups):
        pl.semaphore_signal(barrier, inc=1, device_id={"slab": lax.rem(slab + shift, groups)}, device_id_type=MESH)

    mine = pl.multiple_of(me * frows, 16)
    loads = [
        pltpu.make_async_copy(source, target, load_sem.at[i])
        for i, (source, target) in enumerate((
            (stiff_hbm, stiff_ref),
            (feats_hbm, gathered.at[pl.ds(mine, beads), :]),
            (nbrs_hbm, nbrs_ref),
            (w_hbm, w_ref),
            (order_hbm, order_ref),
        ))
    ]
    for load in loads:
        load.start()
    loads[0].wait()
    stiff = stiff_ref[...]
    high = stiff.astype(jnp.bfloat16).astype(jnp.float32)
    mid = (stiff - high).astype(jnp.bfloat16).astype(jnp.float32)
    low = stiff - high - mid
    parts = jnp.concatenate([high, mid, low], axis=0)
    tail = jnp.concatenate([parts, jnp.zeros((TAIL - parts.shape[0], parts.shape[1]), jnp.float32)], axis=0)
    gathered[pl.ds(mine + beads, TAIL), :] = tail.astype(jnp.bfloat16)
    loads[1].wait()

    if tree:
        pl.semaphore_wait(barrier, len(mates) + groups - 1)
    else:
        pl.semaphore_wait(barrier, n - 1 + groups - 1)

    half = beads // 2
    drain_feats = (short_gather if tree else direct_gather)(n, me, gathered, frows, ((0, half), (half, half + TAIL)), fsend, frecv)
    for load in loads[2:]:
        load.wait()
    for origin in range(n):
        wide[pl.ds(origin * beads, beads), :] = gathered[pl.ds(origin * frows, beads), :].astype(jnp.float32)

    chunk = 16
    first = pl.multiple_of(me * beads, 16)

    def make(piece):
        @pl.loop(piece * half // chunk, (piece + 1) * half // chunk)
        def _(step):
            base = pl.multiple_of(step * chunk, chunk)
            for link in range(links):
                for bead in range(chunk):
                    row = nbrs_ref[link * beads + base + bead]
                    near[pl.ds(link * chunk + bead, 1), :] = wide[pl.ds(row, 1), :]
            own = gathered[pl.ds(pl.multiple_of(mine + base, 16), chunk), :].astype(jnp.float32)
            mixed = near[...].reshape(links, chunk, -1) * own[None]
            mixed = mixed.reshape(links * chunk, -1).astype(jnp.bfloat16)
            pre = jnp.dot(mixed, w_ref[...], preferred_element_type=jnp.float32)
            total = jnp.sum(jnp.tanh(pre).reshape(links, chunk, -1), axis=0)
            slab_ref[pl.ds(first + base, chunk), :] = (total * scale).astype(jnp.bfloat16)

    drain_slab = gather(n, me, slab_ref, beads, ((0, half), (half, half)), ssend, srecv, make)

    home_rows = pl.ds(pl.multiple_of(home * block, 16), block)

    def column_copy(shift):
        return pltpu.make_async_remote_copy(
            src_ref=slab_ref.at[home_rows, :], dst_ref=column_ref, send_sem=csend.at[shift], recv_sem=crecv,
            device_id={"slab": lax.rem(slab + shift, groups)}, device_id_type=MESH,
        )

    @pl.when(slab == owner)
    def _():
        for shift in range(1, groups):
            column_copy(shift).start()
        column_ref[...] = slab_ref[home_rows, :]

    chosen = order_ref[:, 0:1]
    chosen_ref[...] = jnp.broadcast_to(chosen, chosen_ref.shape)
    blocks = slab_ref.shape[0] // block
    passed = [(chosen >= (r + 1) * groups).astype(jnp.int32) for r in range(blocks)]
    number = sum(passed)
    lane = chosen - number * groups

    def mask(flag, lanes):
        return jnp.broadcast_to(flag.astype(jnp.float32), (16, lanes)).astype(jnp.bfloat16)

    channels = slab_ref.shape[1]
    masks = [mask(number == r, channels) for r in range(blocks)]
    for row in range(0, block, 16):
        picked = sum(slab_ref[r * block + row:r * block + row + 16, :] * masks[r] for r in range(blocks))
        pivots[pl.ds(pl.multiple_of(slab * block + row, 16), 16), :] = picked

    def pivot_copy(shift, source):
        part = pivots.at[pl.ds(pl.multiple_of(source * block, 16), block), :]
        return pltpu.make_async_remote_copy(
            src_ref=part, dst_ref=part, send_sem=psend.at[shift], recv_sem=precv.at[shift],
            device_id={"slab": lax.rem(slab + shift, groups)}, device_id_type=MESH,
        )

    for shift in range(1, groups):
        pivot_copy(shift, slab).start()

    for shift in range(1, groups):
        pivot_copy(shift, lax.rem(slab + groups - shift, groups)).wait_recv()
    masks = [mask(lane == g, channels) for g in range(groups)]
    for row in range(0, block, 16):
        pivot_ref[row:row + 16, :] = sum(
            pivots[g * block + row:g * block + row + 16, :] * masks[g] for g in range(groups)
        )
    held = sum(
        gathered[b * frows + beads:(b + 1) * frows, :].astype(jnp.float32)
        * jnp.broadcast_to((chosen == b).astype(jnp.float32), (TAIL, gathered.shape[1]))
        for b in range(n)
    )
    lanes = block // held.shape[1]
    pstiff_ref[...] = held[0:lanes] + held[lanes:2 * lanes] + held[2 * lanes:3 * lanes]

    for shift in range(1, groups):
        pivot_copy(shift, slab).wait_send()

    @pl.when(slab != owner)
    def _():
        column_copy(1).wait_recv()

    @pl.when(slab == owner)
    def _():
        for shift in range(1, groups):
            column_copy(shift).wait_send()

    drain_feats()
    drain_slab()


def as_row(pieces):
    return jnp.concatenate([pieces[i:i + 1, :] for i in range(pieces.shape[0])], axis=1)


def split(value):
    high = value.astype(jnp.bfloat16)
    return high, (value - high.astype(jnp.float32)).astype(jnp.bfloat16)


def dot3(left, right, dims):
    lh, ll = split(left)
    rh, rl = split(right)
    dims = (dims, ((), ()))
    mul = lambda a, b: lax.dot_general(a, b, dims, preferred_element_type=jnp.float32)
    return mul(lh, rh) + (mul(lh, rl) + mul(ll, rh))


def small_inverse(both):
    size, lanes = both.shape
    kept = []
    for start in range(0, size, 8):
        rows = both.shape[0]
        down = lax.broadcasted_iota(jnp.int32, (rows, lanes), 0)
        cols = [jnp.broadcast_to(both[:, start + m:start + m + 1], (rows, lanes)) for m in range(8)]
        for k in range(8):
            ratio = jnp.where(down > k, cols[k] * (1.0 / cols[k][k:k + 1, :]), 0.0)
            for m in range(k + 1, 8):
                cols[m] = cols[m] - ratio * cols[m][k:k + 1, :]
            both = both - ratio * both[k:k + 1, :]
        kept.append(both[:8])
        both = both[8:]
    return jnp.concatenate(kept, axis=0)


def eliminate(fp_ref, pstiff_ref, work, ident, lowinv, log_ref):
    block = fp_ref.shape[0]
    step = 32
    fp = fp_ref[...]
    square = lax.dot_general(fp, fp, (((1,), (1,)), ((), ())), preferred_element_type=jnp.float32)
    rows = lax.broadcasted_iota(jnp.int32, (block, block), 0)
    cols = lax.broadcasted_iota(jnp.int32, (block, block), 1)
    work[...] = square + jnp.where(rows == cols, as_row(pstiff_ref[...]), 0.0)
    ident[...] = (rows == cols).astype(jnp.float32)
    lowinv[...] = jnp.zeros(lowinv.shape, jnp.float32)
    eye = (
        lax.broadcasted_iota(jnp.int32, (step, step), 0) == lax.broadcasted_iota(jnp.int32, (step, step), 1)
    ).astype(jnp.float32)
    logs = jnp.zeros((1, 1), jnp.float32)
    for start in range(0, block, step):
        after = start + step
        both = small_inverse(jnp.concatenate([work[start:after, start:after], eye], axis=1))
        diag = jnp.sum(both[:, :step] * eye, axis=1, keepdims=True)
        logs = logs + jnp.sum(jnp.log(diag), axis=0, keepdims=True)
        inverse = both[:, step:] * lax.rsqrt(diag)
        low = after // 128 * 128
        high = -(-after // 128) * 128
        if after == block:
            lowinv[start:after, :] = dot3(inverse, ident[start:after, :], ((1,), (0,)))
            break
        wide = jnp.concatenate([work[start:after, low:], ident[start:after, :high]], axis=1)
        done = dot3(inverse, wide, ((1,), (0,)))
        lowinv[start:after, :high] = done[:, block - low:]
        change = dot3(done[:, :block - low], done, ((0,), (0,)))
        work[low:, low:] = work[low:, low:] - change[:, :block - low]
        ident[low:, :high] = ident[low:, :high] - change[:, block - low:]
    log_ref[0, 0] = jnp.sum(logs) * (1.0 / (STEPS * block))


def finish_kernel(
    groups, chosen_ref, slab_ref, column_ref, fp_ref, pstiff_ref, stiff_ref,
    out_ref, log_ref, work, ident, lowinv, whigh, wlow, pcol,
):
    me = lax.axis_index("band")
    slab = lax.axis_index("slab")
    r = pl.program_id(0)
    pivot = chosen_ref[...]
    block = fp_ref.shape[0]
    nt = (((1,), (1,)), ((), ()))

    def panel(rows):
        return lax.dot_general(rows, whigh[...], nt, preferred_element_type=jnp.float32) + lax.dot_general(
            rows, wlow[...], nt, preferred_element_type=jnp.float32
        )

    @pl.when(r == 0)
    def _():
        eliminate(fp_ref, pstiff_ref, work, ident, lowinv, log_ref)
        ih, il = split(lowinv[...])
        fp = fp_ref[...]
        w = jnp.dot(ih, fp, preferred_element_type=jnp.float32) + jnp.dot(
            il, fp, preferred_element_type=jnp.float32
        )
        whigh[...], wlow[...] = split(w)
        pcol[...] = jnp.where(me == pivot, 0.0, panel(column_ref[...])).astype(jnp.bfloat16)

    here = r * groups + slab
    rows = slab_ref[...]
    own = jnp.where(here == pivot, 0.0, panel(rows)).astype(jnp.bfloat16)
    value = lax.dot_general(rows, column_ref[...], nt, preferred_element_type=jnp.float32)
    value = value - lax.dot_general(own, pcol[...], nt, preferred_element_type=jnp.float32)
    iota = [lax.broadcasted_iota(jnp.int32, value.shape, d) for d in (0, 1)]
    on = jnp.logical_and(iota[0] == iota[1], here == me)
    value = value + jnp.where(on, as_row(stiff_ref[...]), 0.0)
    parts = block // 128
    for part in range(parts):
        out_ref[pl.ds(part, block, stride=parts), :] = value[:, part * 128:(part + 1) * 128]


def on_device(n, groups, feats, nbrs, w_pair, stiff, order):
    own_feats = feats[0]
    beads, width = own_feats.shape
    links = nbrs.shape[2]
    channels = w_pair.shape[1]
    block = stiff.shape[0]
    count = n * beads
    flat = nbrs[0].T.reshape(links * beads)
    stiff2 = stiff.reshape(block // 128, 128)
    scale = 1.5 / math.sqrt(links * channels)
    vmem = pl.BlockSpec(memory_space=pltpu.VMEM)
    hbm = pl.BlockSpec(memory_space=pltpu.HBM)
    dma = pltpu.SemaphoreType.DMA
    slab_factor, column, pivot_factor, pivot_stiff, own_stiff, chosen = pl.pallas_call(
        functools.partial(assemble_kernel, n, groups, block, scale),
        out_shape=(
            jax.ShapeDtypeStruct((count, channels), jnp.bfloat16),
            jax.ShapeDtypeStruct((block, channels), jnp.bfloat16),
            jax.ShapeDtypeStruct((block, channels), jnp.bfloat16),
            jax.ShapeDtypeStruct((block // 128, 128), jnp.float32),
            jax.ShapeDtypeStruct((block // 128, 128), jnp.float32),
            jax.ShapeDtypeStruct((1, block), jnp.int32),
        ),
        in_specs=[hbm] * 5,
        out_specs=(vmem,) * 6,
        scratch_shapes=[
            pltpu.VMEM((1, order.shape[0]), jnp.int32),
            pltpu.SMEM((links * beads,), jnp.int32),
            pltpu.VMEM((width, channels), jnp.bfloat16),
            dma((5,)),
            pltpu.VMEM((n * (beads + TAIL), width), jnp.bfloat16),
            pltpu.VMEM((count, width), jnp.float32),
            pltpu.VMEM((links * 16, width), jnp.float32),
            pltpu.VMEM((groups * block, channels), jnp.bfloat16),
            dma((n * 8,)), dma((n * 2,)), dma((n * 8,)), dma((n * 2,)),
            dma((groups,)), dma(()), dma((groups,)), dma((groups,)),
        ],
        compiler_params=pltpu.CompilerParams(
            collective_id=0, has_side_effects=True, vmem_limit_bytes=60 * 1024 * 1024
        ),
        name="assemble",
    )(order.reshape(1, -1), flat, own_feats, w_pair, stiff2)

    whole = lambda shape: pl.BlockSpec(shape, lambda r: (0,) * len(shape))
    out, logs = pl.pallas_call(
        functools.partial(finish_kernel, groups),
        grid=(count // block,),
        out_shape=(
            jax.ShapeDtypeStruct((count * block // 128, 128), jnp.float32),
            jax.ShapeDtypeStruct((1, 1), jnp.float32),
        ),
        in_specs=[
            whole((1, block)),
            pl.BlockSpec((block, channels), lambda r: (r, 0)),
            whole((block, channels)), whole((block, channels)),
            whole((block // 128, 128)), whole((block // 128, 128)),
        ],
        out_specs=(
            pl.BlockSpec((block * block // 128, 128), lambda r: (r, 0)),
            pl.BlockSpec(memory_space=pltpu.SMEM),
        ),
        scratch_shapes=[
            pltpu.VMEM((block, block), jnp.float32),
            pltpu.VMEM((block, block), jnp.float32),
            pltpu.VMEM((block, block), jnp.float32),
            pltpu.VMEM((block, channels), jnp.bfloat16),
            pltpu.VMEM((block, channels), jnp.bfloat16),
            pltpu.VMEM((block, block), jnp.bfloat16),
        ],
        compiler_params=pltpu.CompilerParams(vmem_limit_bytes=60 * 1024 * 1024),
        name="finish",
    )(chosen, slab_factor, column, pivot_factor, pivot_stiff, own_stiff)
    return out.reshape(1, count, 1, block), logs[0, 0]


def solution(mesh):
    in_specs = (P("slab", "band", None), P("slab", "band", None), P(), P("band"), P())
    out_specs = (P("slab", None, "band", None), P())
    return jax.shard_map(
        functools.partial(on_device, mesh.shape["band"], mesh.shape["slab"]),
        mesh=mesh, in_specs=in_specs, out_specs=out_specs, check_vma=False,
    )
```
